256 devices in a mesh: shot: 8 (over z), rx: 4 (over y), ry: 8 (over x, core).
Axes of the slice: x: 4, y: 4, z: 8, core: 2. Of those that a mesh axis runs over, the one named last changes fastest.
Arguments:
- traces: bfloat16 [1024, 1024, 1024], P('shot', ('rx', 'ry')), may hold values from -6 to 6
- ghost_filter: bfloat16 [64], replicated, may hold values from -0.75 to 0.75
- bands: int32 [64], replicated, may hold values from 1 to 511
Outputs:
- multiples: float32 [64, 2, 1024, 1024], P('shot', None, 'ry', 'rx')
The draws below stay inside these ranges and needn't reach their ends.
All inputs are finite; a program needn't handle non-finite values.
Results may differ from the reference program's by a relative error of at most 0.0055.
Values may be sent and summed in bfloat16 or wider, within the bound.
No kernel may reach another device: no remote copies, remote signals or barrier semaphores. Data moves between devices by JAX's collectives and lax.ppermute only.
A program may use at most 128 MiB of HBM per device.

```python
import math
import jax
import jax.numpy as jnp
from jax import lax

ORDER = 1024
NT = 1024
TAPS = 64
BANDS = 64


def with_ends(result, key, low, high):
    longest = result.shape.index(max(result.shape))
    spots = []
    for shift in (0, 1):
        where = [jax.random.randint(jax.random.fold_in(key, axis), (), 0, length) for axis, length in enumerate(result.shape)]
        where[longest] = (where[longest] + shift) % result.shape[longest]
        spots.append(tuple(where))
    return result.at[spots[0]].set(low).at[spots[1]].set(high)


def steps_of(key, shape, pieces, low, top_value):
    def one(axis_at, parts):
        draws = jax.random.uniform(jax.random.fold_in(jax.random.fold_in(key, 6), axis_at), (parts,), jnp.float32, low / len(pieces), top_value / len(pieces))
        return jnp.repeat(jnp.exp(draws), shape[axis_at] // parts).reshape((-1,) + (1,) * (len(shape) - axis_at - 1))

    gain = one(*pieces[0])
    for cut in pieces[1:]:
        gain = gain * one(*cut)
    return gain


def scatter_about(rng, shape, scale, reach, shards=(), kind=jnp.bfloat16):
    drawn = jax.random.normal(rng, shape, jnp.float32) * scale
    if len(shards) > 0:
        drawn = steps_of(rng, shape, shards, -0.22, 0.18) * drawn
    return jnp.clip(drawn, min=-reach, max=reach).astype(kind)


def setup_inputs(seed: int = 0) -> dict:
    seeds = jax.random.split(jax.random.key(seed), 4)
    return {
        "traces": scatter_about(seeds[0], (ORDER, ORDER, NT), 1.0, 6.0, ((0, 8), (1, 32))),
        "ghost_filter": scatter_about(seeds[1], (TAPS,), TAPS ** -0.5, 0.75),
        "bands": with_ends(jax.random.randint(seeds[2], (BANDS,), 1, NT // 2), jax.random.fold_in(seeds[2], 1), 1, (NT // 2) - 1).astype(jnp.int32),
    }


def make_table(bands):
    phase = jnp.arange(NT, dtype=jnp.int32)[:, None] * bands[None, :] % NT
    angle = 2.0 * math.pi / NT * phase.astype(jnp.float32)
    table = jnp.concatenate([jnp.cos(angle), -jnp.sin(angle)], 1) * (1.0 / math.sqrt(NT))
    return table.astype(jnp.bfloat16)

def front_end(shot_traces, taps, table):
    signal = shot_traces.astype(jnp.float32)
    length = 2 * NT
    spectrum = jnp.fft.rfft(signal, length, axis=-1) * jnp.fft.rfft(taps, length)
    convolved = jnp.fft.irfft(spectrum, length, axis=-1)[:, :NT]
    deghosted = convolved.astype(jnp.bfloat16)
    picked = jnp.dot(deghosted, table, preferred_element_type=jnp.float32)
    count = table.shape[1] // 2
    return jnp.stack([picked[:, :count], picked[:, count:]]).astype(jnp.bfloat16)

def square_band(matrix):
    real_part = matrix[0]
    imag_part = matrix[1]
    rr = jnp.dot(real_part, real_part, preferred_element_type=jnp.float32)
    ii = jnp.dot(imag_part, imag_part, preferred_element_type=jnp.float32)
    ri = jnp.dot(real_part, imag_part, preferred_element_type=jnp.float32)
    ir = jnp.dot(imag_part, real_part, preferred_element_type=jnp.float32)
    factor = -1.0 / math.sqrt(ORDER)
    return jnp.stack([(rr - ii) * factor, (ri + ir) * factor])

def reference(traces, ghost_filter, bands):
    taps = ghost_filter.astype(jnp.float32)
    table = make_table(bands)
    spectra = lax.map(lambda shot_traces: front_end(shot_traces, taps, table), traces)
    spectra = jnp.transpose(spectra, (3, 1, 0, 2))
    return lax.map(square_band, spectra)
```

```python
import functools
import math

import jax
import jax.numpy as jnp
from jax import lax
from jax.experimental import pallas as pl
from jax.experimental.pallas import tpu as pltpu
from jax.sharding import PartitionSpec as P

CHUNKS = 1
VMEM_LIMIT = 56 * 1024 * 1024


def filter_table(taps_ref, bands_ref, weights_ref, table_ref):
    samples = weights_ref.shape[0]
    taps = taps_ref.shape[1]
    bands = bands_ref[...]
    count = bands.shape[1]
    both = jnp.concatenate([bands, bands], 1)
    first = lax.broadcasted_iota(jnp.int32, (1, 2 * count), 1) < count
    step = 32
    index = lax.broadcasted_iota(jnp.int32, (step, 2 * count), 0)

    def angle_of(times):
        phase = lax.rem(times * both, samples)
        return (2.0 * math.pi / samples) * phase.astype(jnp.float32)

    coarse = angle_of(index * step)
    fine = angle_of(index)
    coarse_cos, coarse_sin = jnp.cos(coarse), jnp.sin(coarse)
    scale = 1.0 / math.sqrt(samples)
    fine_cos, fine_sin = jnp.cos(fine) * scale, jnp.sin(fine) * scale
    first_part = jnp.where(first, coarse_cos, -coarse_sin)
    second_part = jnp.where(first, coarse_sin, coarse_cos)
    for block in range(samples // step):
        rows = (
            first_part[block : block + 1] * fine_cos - second_part[block : block + 1] * fine_sin
        )
        table_ref[block * step : (block + 1) * step, :] = rows.astype(jnp.bfloat16)
    table_ref[samples:, :] = jnp.zeros((table_ref.shape[0] - samples, 2 * count), jnp.bfloat16)

    block = 128
    padded = jnp.concatenate(
        [taps_ref[...].astype(jnp.float32), jnp.zeros((1, 2 * block - taps), jnp.float32)], 1
    )
    band_matrix = pltpu.roll(
        jnp.broadcast_to(padded, (block, 2 * block)), 0, 1, stride=1, stride_axis=0
    ).astype(jnp.bfloat16)
    for at in range(samples // block):
        filtered = jnp.dot(
            band_matrix,
            table_ref[at * block : (at + 2) * block, :],
            preferred_element_type=jnp.float32,
        )
        high = filtered.astype(jnp.bfloat16)
        low = (filtered - high.astype(jnp.float32)).astype(jnp.bfloat16)
        weights_ref[at * block : (at + 1) * block, : 2 * count] = high
        weights_ref[at * block : (at + 1) * block, 2 * count :] = low


def front_kernel(
    place_ref, taps_ref, bands_ref, traces_ref, *rest, chunks, planes, owned
):
    outs = rest[: 2 * chunks]
    weights_ref, table_ref, picked_ref, turned_ref = rest[2 * chunks :]
    shots, receivers, samples = traces_ref.shape
    count = bands_ref.shape[1]

    @pl.when(pl.program_id(0) == 0)
    def _():
        filter_table(taps_ref, bands_ref, weights_ref, table_ref)

    group = 16
    for at in range(shots // group):
        block = traces_ref[at * group : (at + 1) * group].reshape(group * receivers, samples)
        both = jnp.dot(block, weights_ref[...], preferred_element_type=jnp.float32)
        picked_ref[at * group * receivers : (at + 1) * group * receivers, :] = (
            both[:, : 2 * count] + both[:, 2 * count :]
        )
    for receiver in range(receivers):
        turned_ref[receiver * 2 * count : (receiver + 1) * 2 * count, :] = picked_ref[
            pl.ds(receiver, shots, stride=receivers), :
        ].T
    plane, core = place_ref[0], place_ref[1]
    half = owned // 2
    per_chunk = half // chunks
    for other in range(2):
        for hop in range(planes):
            base = lax.rem(plane + hop, planes) * owned + (core ^ other) * half
            for part in range(2):
                for band in range(half):
                    lane = base + (part * count + band)
                    rows = turned_ref[pl.ds(lane, receivers, stride=2 * count), :]
                    outs[other * chunks + band // per_chunk][
                        hop, part * per_chunk + band % per_chunk
                    ] = rows.astype(jnp.bfloat16)


def front(place, taps, bands, traces, chunks, planes):
    shots, receivers, samples = traces.shape
    count = bands.shape[0]
    owned = count // planes
    block = 16
    per_chunk = owned // chunks
    out = jax.ShapeDtypeStruct((planes, per_chunk, receivers, shots), jnp.bfloat16)
    out_spec = pl.BlockSpec((planes, per_chunk, block, shots), lambda i, place: (0, 0, i, 0))
    return pl.pallas_call(
        functools.partial(front_kernel, chunks=chunks, planes=planes, owned=owned),
        out_shape=[out] * (2 * chunks),
        grid_spec=pltpu.PrefetchScalarGridSpec(
            num_scalar_prefetch=1,
            grid=(receivers // block,),
            in_specs=[
                pl.BlockSpec((1, taps.shape[0]), lambda i, place: (0, 0)),
                pl.BlockSpec((1, count), lambda i, place: (0, 0)),
                pl.BlockSpec((shots, block, samples), lambda i, place: (0, i, 0)),
            ],
            out_specs=[out_spec] * (2 * chunks),
            scratch_shapes=[
                pltpu.VMEM((samples, 4 * count), jnp.bfloat16),
                pltpu.VMEM((samples + 128, 2 * count), jnp.bfloat16),
                pltpu.VMEM((shots * block, 2 * count), jnp.float32),
                pltpu.VMEM((block * 2 * count, shots), jnp.float32),
            ],
        ),
        compiler_params=pltpu.CompilerParams(vmem_limit_bytes=VMEM_LIMIT),
        cost_estimate=pl.CostEstimate(
            flops=4 * shots * receivers * samples * count * 2,
            bytes_accessed=shots * receivers * samples * 2,
            transcendentals=0,
        ),
        name="front",
    )(place, taps.reshape(1, -1), bands.reshape(1, -1), traces)


UP = ((6, 2), (0, 2), (4, 2))
DOWN = ((1, 3), (0, 1), (4, 2))


def sort_kernel(place_ref, *refs):
    pieces = refs[:8]
    own, up_turn, down_turn, far_turn, up, down, held, sems = refs[8:]
    plane, chip = place_ref[0], place_ref[2]

    def start(copies):
        for copy in copies:
            copy.start()
        for copy in copies:
            copy.wait()

    start(
        [
            pltpu.make_async_copy(
                piece, held.at[lax.rem(plane - hop - 2 * chip + 16, 8)], sems.at[hop]
            )
            for hop, piece in enumerate(pieces)
        ]
    )
    moves = [
        (0, 2, own, 0),
        (2, 2, up_turn, 0),
        (6, 2, down_turn, 0),
        (4, 2, far_turn, 0),
    ]
    for target, order in ((up, UP), (down, DOWN)):
        at = 0
        for first, size in order:
            moves.append((first, size, target, at))
            at += size
    start(
        [
            pltpu.make_async_copy(
                held.at[pl.ds(first, size)], target.at[pl.ds(at, size)], sems.at[number]
            )
            for number, (first, size, target, at) in enumerate(moves)
        ]
    )


def sort_blocks(place, pieces):
    shape = pieces[0].shape
    two = jax.ShapeDtypeStruct((2,) + shape, jnp.bfloat16)
    six = jax.ShapeDtypeStruct((6,) + shape, jnp.bfloat16)
    hbm = pl.BlockSpec(memory_space=pl.ANY)
    return pl.pallas_call(
        sort_kernel,
        out_shape=[two, two, two, two, six, six],
        in_specs=[pl.BlockSpec(memory_space=pltpu.SMEM)] + [hbm] * 8,
        out_specs=[hbm] * 6,
        scratch_shapes=[
            pltpu.VMEM((8,) + shape, jnp.bfloat16),
            pltpu.SemaphoreType.DMA((10,)),
        ],
        compiler_params=pltpu.CompilerParams(vmem_limit_bytes=4 * 1024 * 1024),
        cost_estimate=pl.CostEstimate(flops=0, bytes_accessed=4 << 20, transcendentals=0),
        name="sort",
    )(place, *pieces)


def product_kernel(place_ref, *refs, bands):
    pieces = refs[:8]
    up_turn, down_turn, far_turn, up, down, up_far, down_far = refs[8:15]
    left_own, left_up, left_down, left_up_far, left_down_far = refs[15:20]
    keep_ref, give_ref, right, left, sems = refs[20:]
    plane, core, chip, column = (place_ref[i] for i in range(4))
    width = pieces[0].shape[1]
    copies = []

    def copy(source, target):
        copies.append(pltpu.make_async_copy(source, target, sems.at[len(copies)]))

    def into_right(source, first, size, target_chip):
        block = lax.rem(2 * target_chip + first, 8)
        start = pl.multiple_of(target_chip * width, width)
        copy(source, right.at[pl.ds(block, size), :, pl.ds(start, width), :])

    for hop, piece in enumerate(pieces):
        copy(
            piece,
            right.at[
                lax.rem(plane - hop + 8, 8), :, pl.ds(pl.multiple_of(chip * width, width), width), :
            ],
        )
    below, above, across = lax.rem(chip + 3, 4), lax.rem(chip + 1, 4), lax.rem(chip + 2, 4)
    into_right(up_turn, 2, 2, below)
    into_right(down_turn, 6, 2, above)
    into_right(far_turn, 4, 2, across)
    for source, order, target_chip in ((up, UP, below), (down, DOWN, above)):
        at = 0
        for first, size in order:
            while size:
                step = min(size, 2 - first % 2)
                into_right(source.at[pl.ds(at, step)], first, step, target_chip)
                at, first, size = at + step, first + step, size - step
    for source, order in ((up_far, UP), (down_far, DOWN)):
        at = 0
        for first, size in order:
            while size and at < 3:
                step = min(size, 2 - first % 2, 3 - at)
                into_right(source.at[pl.ds(at, step)], first, step, across)
                at, first, size = at + step, first + step, size - step
    chips = (chip, below, above, across)
    for source, slots, hop in (
        (left_own, range(4), 0),
        (left_up, range(4), 3),
        (left_down, range(4), 1),
        (left_up_far, range(2), 2),
        (left_down_far, range(2, 4), 2),
    ):
        for at, slot in enumerate(slots):
            start = lax.rem(column + hop, 4) * 4 * width + chips[slot] * width
            copy(
                source.at[at],
                left.at[:, :, pl.ds(pl.multiple_of(start, width), width), :],
            )
    for one in copies:
        one.start()
    for one in copies:
        one.wait()

    order = 8 * 128
    factor = -1.0 / math.sqrt(order)
    for band in range(bands):
        rows = [
            jnp.concatenate([right[z, part * bands + band] for z in range(8)], 1)
            for part in range(2)
        ]
        columns = [
            jnp.concatenate([left[s, part * bands + band] for s in range(2)], 1)
            for part in range(2)
        ]

        def times(a, b):
            return jnp.dot(rows[a], columns[b], preferred_element_type=jnp.float32)

        for part, value in enumerate(
            (times(0, 0) - times(1, 1), times(0, 1) + times(1, 0))
        ):
            turned = (value * factor).T
            low, high = turned[:128], turned[128:]
            keep_ref[band, part] = jnp.where(core == 0, low, high)
            give_ref[band, part] = jnp.where(core == 0, high, low)


def product(place, pieces, rest):
    parts, width, shots = pieces[0].shape
    bands = parts // 2
    receivers = 4 * width
    hbm = pl.BlockSpec(memory_space=pl.ANY)
    out = jax.ShapeDtypeStruct((bands, 2, shots, receivers), jnp.float32)
    return pl.pallas_call(
        functools.partial(product_kernel, bands=bands),
        out_shape=[out, out],
        in_specs=[pl.BlockSpec(memory_space=pltpu.SMEM)] + [hbm] * 20,
        scratch_shapes=[
            pltpu.VMEM((8, parts, receivers, shots), jnp.bfloat16),
            pltpu.VMEM((2, parts, 4 * receivers, shots), jnp.bfloat16),
            pltpu.SemaphoreType.DMA((64,)),
        ],
        compiler_params=pltpu.CompilerParams(vmem_limit_bytes=32 * 1024 * 1024),
        cost_estimate=pl.CostEstimate(
            flops=8 * bands * receivers * receivers * 1024,
            bytes_accessed=24 << 20,
            transcendentals=0,
        ),
        name="product",
    )(place, *pieces, *rest)


def local(traces, ghost_filter, bands):
    plane = lax.axis_index("shot")
    column = lax.axis_index("rx")
    row = lax.axis_index("ry")
    core, chip = row % 2, row // 2
    place = jnp.stack([plane, core, chip, column]).astype(jnp.int32)
    planes = 8
    fronts = front(place, ghost_filter, bands, traces, CHUNKS, planes)
    mine, others = fronts[:CHUNKS], fronts[CHUNKS:]

    def along_x(value, hop):
        pairs = [(i, ((i // 2 + hop) % 4) * 2 + i % 2) for i in range(8)]
        return lax.ppermute(value, "ry", pairs)

    def along_y(value, hop):
        return lax.ppermute(value, "rx", [(i, (i + hop) % 4) for i in range(4)])

    def along_z(value, hop):
        return lax.ppermute(value, "shot", [(i, (i + hop) % planes) for i in range(planes)])

    def swap(value):
        return lax.ppermute(value, "ry", [(i, i ^ 1) for i in range(8)])

    keeps, takes = [], []
    for chunk in range(CHUNKS):
        own = mine[chunk]
        theirs = swap(others[chunk])
        low = jnp.where(core == 0, own, theirs)
        high = jnp.where(core == 0, theirs, own)
        pieces = []
        for hop in range(planes):
            piece = jnp.concatenate([low[hop], high[hop]], 1)
            pieces.append(along_z(piece, hop) if hop else piece)
        own_turn, up_turn, down_turn, far_turn, up, down = sort_blocks(place, pieces)
        up_turn, down_turn, far_turn = (
            along_x(up_turn, 1),
            along_x(down_turn, -1),
            along_x(far_turn, 2),
        )
        up, down = along_x(up, 1), along_x(down, -1)
        up_far, down_far = along_x(up[:3], 1), along_x(down[:3], -1)
        left = jnp.stack([own_turn, up_turn, down_turn, far_turn])
        left_up, left_down = along_y(left, 1), along_y(left, -1)
        left_up_far, left_down_far = along_y(left_up[:2], 1), along_y(left_down[2:], -1)
        keep, give = product(
            place,
            pieces,
            (up_turn, down_turn, far_turn, up, down, up_far, down_far)
            + (left, left_up, left_down, left_up_far, left_down_far),
        )
        keeps.append(keep)
        takes.append(swap(give))
    return jnp.where(
        core == 0,
        jnp.concatenate(keeps + takes),
        jnp.concatenate(takes + keeps),
    )


def solution(mesh):
    placed = (P("shot", ("rx", "ry"), None), P(), P())
    return jax.shard_map(
        local, mesh=mesh, in_specs=placed, out_specs=P("shot", None, "ry", "rx"), check_vma=False
    )
```

```python
import functools
import math

import jax
import jax.numpy as jnp
from jax import lax
from jax.experimental import pallas as pl
from jax.experimental.pallas import tpu as pltpu
from jax.sharding import PartitionSpec as P

CHUNKS = 1
ZORDER = (3, 5, 4, 2, 6, 1, 7, 0)
VMEM_LIMIT = 56 * 1024 * 1024


def filter_table(taps_ref, bands_ref, weights_ref, table_ref):
    samples = weights_ref.shape[0]
    taps = taps_ref.shape[1]
    bands = bands_ref[...]
    count = bands.shape[1]
    both = jnp.concatenate([bands, bands], 1)
    first = lax.broadcasted_iota(jnp.int32, (1, 2 * count), 1) < count
    step = 32
    index = lax.broadcasted_iota(jnp.int32, (step, 2 * count), 0)

    def angle_of(times):
        phase = lax.rem(times * both, samples)
        return (2.0 * math.pi / samples) * phase.astype(jnp.float32)

    coarse = angle_of(index * step)
    fine = angle_of(index)
    coarse_cos, coarse_sin = jnp.cos(coarse), jnp.sin(coarse)
    scale = 1.0 / math.sqrt(samples)
    fine_cos, fine_sin = jnp.cos(fine) * scale, jnp.sin(fine) * scale
    first_part = jnp.where(first, coarse_cos, -coarse_sin)
    second_part = jnp.where(first, coarse_sin, coarse_cos)
    for block in range(samples // step):
        rows = (
            first_part[block : block + 1] * fine_cos - second_part[block : block + 1] * fine_sin
        )
        table_ref[block * step : (block + 1) * step, :] = rows.astype(jnp.bfloat16)
    table_ref[samples:, :] = jnp.zeros((table_ref.shape[0] - samples, 2 * count), jnp.bfloat16)

    block = 128
    padded = jnp.concatenate(
        [taps_ref[...].astype(jnp.float32), jnp.zeros((1, 2 * block - taps), jnp.float32)], 1
    )
    band_matrix = pltpu.roll(
        jnp.broadcast_to(padded, (block, 2 * block)), 0, 1, stride=1, stride_axis=0
    ).astype(jnp.bfloat16)
    for at in range(samples // block):
        filtered = jnp.dot(
            band_matrix,
            table_ref[at * block : (at + 2) * block, :],
            preferred_element_type=jnp.float32,
        )
        high = filtered.astype(jnp.bfloat16)
        low = (filtered - high.astype(jnp.float32)).astype(jnp.bfloat16)
        weights_ref[at * block : (at + 1) * block, : 2 * count] = high
        weights_ref[at * block : (at + 1) * block, 2 * count :] = low


def front_kernel(
    place_ref, taps_ref, bands_ref, traces_ref, *rest, chunks, planes, owned
):
    outs = rest[: 2 * chunks]
    weights_ref, table_ref, picked_ref, turned_ref = rest[2 * chunks :]
    shots, receivers, samples = traces_ref.shape
    count = bands_ref.shape[1]

    @pl.when(pl.program_id(0) == 0)
    def _():
        filter_table(taps_ref, bands_ref, weights_ref, table_ref)

    group = 16
    for at in range(shots // group):
        block = traces_ref[at * group : (at + 1) * group].reshape(group * receivers, samples)
        both = jnp.dot(block, weights_ref[...], preferred_element_type=jnp.float32)
        picked_ref[at * group * receivers : (at + 1) * group * receivers, :] = (
            both[:, : 2 * count] + both[:, 2 * count :]
        )
    for receiver in range(receivers):
        turned_ref[receiver * 2 * count : (receiver + 1) * 2 * count, :] = picked_ref[
            pl.ds(receiver, shots, stride=receivers), :
        ].T
    plane, core = place_ref[0], place_ref[1]
    half = owned // 2
    per_chunk = half // chunks
    for other in range(2):
        for hop in range(planes):
            base = lax.rem(plane + hop, planes) * owned + (core ^ other) * half
            for part in range(2):
                for band in range(half):
                    lane = base + (part * count + band)
                    rows = turned_ref[pl.ds(lane, receivers, stride=2 * count), :]
                    outs[other * chunks + band // per_chunk][
                        hop, part * per_chunk + band % per_chunk
                    ] = rows.astype(jnp.bfloat16)


def front(place, taps, bands, traces, chunks, planes):
    shots, receivers, samples = traces.shape
    count = bands.shape[0]
    owned = count // planes
    block = 16
    per_chunk = owned // chunks
    out = jax.ShapeDtypeStruct((planes, per_chunk, receivers, shots), jnp.bfloat16)
    out_spec = pl.BlockSpec((planes, per_chunk, block, shots), lambda i, place: (0, 0, i, 0))
    return pl.pallas_call(
        functools.partial(front_kernel, chunks=chunks, planes=planes, owned=owned),
        out_shape=[out] * (2 * chunks),
        grid_spec=pltpu.PrefetchScalarGridSpec(
            num_scalar_prefetch=1,
            grid=(receivers // block,),
            in_specs=[
                pl.BlockSpec((1, taps.shape[0]), lambda i, place: (0, 0)),
                pl.BlockSpec((1, count), lambda i, place: (0, 0)),
                pl.BlockSpec((shots, block, samples), lambda i, place: (0, i, 0)),
            ],
            out_specs=[out_spec] * (2 * chunks),
            scratch_shapes=[
                pltpu.VMEM((samples, 4 * count), jnp.bfloat16),
                pltpu.VMEM((samples + 128, 2 * count), jnp.bfloat16),
                pltpu.VMEM((shots * block, 2 * count), jnp.float32),
                pltpu.VMEM((block * 2 * count, shots), jnp.float32),
            ],
        ),
        compiler_params=pltpu.CompilerParams(vmem_limit_bytes=VMEM_LIMIT),
        cost_estimate=pl.CostEstimate(
            flops=4 * shots * receivers * samples * count * 2,
            bytes_accessed=shots * receivers * samples * 2,
            transcendentals=0,
        ),
        name="front",
    )(place, taps.reshape(1, -1), bands.reshape(1, -1), traces)


UP = ((6, 2), (0, 2), (4, 2))
DOWN = ((1, 3), (0, 1), (4, 2))


def sort_kernel(place_ref, *refs):
    pieces = refs[:8]
    held = refs[8]
    turns = refs[9:]
    first = place_ref[0] - 2 * place_ref[2] + 8
    for hop, piece in zip(ZORDER, pieces):
        held[lax.rem(first - hop + 8, 8)] = piece[...]
    for pair, turn in enumerate(turns):
        turn[...] = held[2 * pair : 2 * pair + 2]


def sort_blocks(place, pieces):
    shape = pieces[0].shape
    two = jax.ShapeDtypeStruct((2,) + shape, jnp.bfloat16)
    eight = jax.ShapeDtypeStruct((8,) + shape, jnp.bfloat16)
    vmem = pl.BlockSpec(memory_space=pltpu.VMEM)
    return pl.pallas_call(
        sort_kernel,
        out_shape=[eight, two, two, two, two],
        in_specs=[pl.BlockSpec(memory_space=pltpu.SMEM)] + [vmem] * 8,
        out_specs=[vmem] * 5,
        compiler_params=pltpu.CompilerParams(vmem_limit_bytes=16 * 1024 * 1024),
        cost_estimate=pl.CostEstimate(flops=0, bytes_accessed=1 << 20, transcendentals=0),
        name="sort",
    )(place, *[pieces[hop] for hop in ZORDER])


def second_kernel(held, up_turn, down_turn, far_turn, after_up, after_down, up, down, turned):
    del after_up, after_down
    for target, order in ((up, UP), (down, DOWN)):
        at = 0
        for first, size in order:
            target[at : at + size] = held[first : first + size]
            at += size
    for at, turn in enumerate((up_turn, down_turn, far_turn)):
        turned[at] = turn[...]


def second_step(held, turns, after):
    block = held.shape[1:]
    six = jax.ShapeDtypeStruct((6,) + block, jnp.bfloat16)
    turned = jax.ShapeDtypeStruct((3, 2) + block, jnp.bfloat16)
    vmem = pl.BlockSpec(memory_space=pltpu.VMEM)
    hbm = pl.BlockSpec(memory_space=pl.ANY)
    return pl.pallas_call(
        second_kernel,
        out_shape=[six, six, turned],
        in_specs=[vmem] * 4 + [hbm] * 2,
        out_specs=[vmem] * 3,
        compiler_params=pltpu.CompilerParams(vmem_limit_bytes=16 * 1024 * 1024),
        cost_estimate=pl.CostEstimate(flops=0, bytes_accessed=1 << 20, transcendentals=0),
        name="second",
    )(held, *turns, *after)


def third_kernel(y_up, y_down, own_down, x_up, x_down, y_up_far, y_down_far, x_up_far, x_down_far):
    y_up_far[...] = y_up[:2]
    y_down_far[0] = own_down[...]
    y_down_far[1] = y_down[2]
    x_up_far[...] = x_up[:3]
    x_down_far[...] = x_down[:3]


def third_step(y_up, y_down, own_down, x_up, x_down):
    block = x_up.shape[1:]
    two = jax.ShapeDtypeStruct((2, 2) + block, jnp.bfloat16)
    three = jax.ShapeDtypeStruct((3,) + block, jnp.bfloat16)
    vmem = pl.BlockSpec(memory_space=pltpu.VMEM)
    return pl.pallas_call(
        third_kernel,
        out_shape=[two, two, three, three],
        in_specs=[vmem] * 5,
        out_specs=[vmem] * 4,
        compiler_params=pltpu.CompilerParams(vmem_limit_bytes=16 * 1024 * 1024),
        cost_estimate=pl.CostEstimate(flops=0, bytes_accessed=1 << 20, transcendentals=0),
        name="third",
    )(y_up, y_down, own_down, x_up, x_down)


LEFTS = (
    (2, (1, 2)),
    (2, (0, 3)),
    (3, (1, 2, 3)),
    (1, (1, 2, 3)),
    (3, (0,)),
    (1, (0,)),
    (0, (0,)),
    (0, (1, 2, 3)),
)


def product_kernel(place_ref, *refs, bands):
    lefts = refs[: len(LEFTS)]
    turned = refs[len(LEFTS) - 1]
    held, up, down, up_far, down_far = refs[len(LEFTS) : -5]
    keep_ref, give_ref, right, left, sems = refs[-5:]
    plane, core, chip, column = (place_ref[i] for i in range(4))
    width = held.shape[2]
    copies = []

    def copy(source, target):
        copies.append(pltpu.make_async_copy(source, target, sems.at[len(copies)]))

    def into_right(source, first, size, target_chip):
        block = lax.rem(2 * target_chip + first, 8)
        start = pl.multiple_of(target_chip * width, width)
        copy(source, right.at[pl.ds(block, size), :, pl.ds(start, width), :])

    for pair in range(4):
        into_right(held.at[pl.ds(2 * pair, 2)], 2 * pair, 2, chip)
    below, above, across = lax.rem(chip + 3, 4), lax.rem(chip + 1, 4), lax.rem(chip + 2, 4)
    into_right(turned.at[0], 2, 2, below)
    into_right(turned.at[1], 6, 2, above)
    into_right(turned.at[2], 4, 2, across)
    for source, order, target_chip in ((up, UP, below), (down, DOWN, above)):
        at = 0
        for first, size in order:
            while size:
                step = min(size, 2 - first % 2)
                into_right(source.at[pl.ds(at, step)], first, step, target_chip)
                at, first, size = at + step, first + step, size - step
    for source, order in ((up_far, UP), (down_far, DOWN)):
        at = 0
        for first, size in order:
            while size and at < 3:
                step = min(size, 2 - first % 2, 3 - at)
                into_right(source.at[pl.ds(at, step)], first, step, across)
                at, first, size = at + step, first + step, size - step
    chips = (chip, below, above, across)
    for source, (hop, slots) in zip(lefts, LEFTS):
        for at, slot in enumerate(slots):
            start = lax.rem(column + hop, 4) * 4 * width + chips[slot] * width
            target = left.at[:, :, pl.ds(pl.multiple_of(start, width), width), :]
            copy(source.at[at] if len(slots) > 1 else source, target)
    for one in copies:
        one.start()
    for one in copies:
        one.wait()

    order = 8 * 128
    factor = -1.0 / math.sqrt(order)
    for band in range(bands):
        rows = [
            jnp.concatenate([right[z, part * bands + band] for z in range(8)], 1)
            for part in range(2)
        ]
        columns = [
            jnp.concatenate([left[s, part * bands + band] for s in range(2)], 1)
            for part in range(2)
        ]

        def times(a, b):
            return jnp.dot(rows[a], columns[b], preferred_element_type=jnp.float32)

        for part, value in enumerate(
            (times(0, 0) - times(1, 1), times(0, 1) + times(1, 0))
        ):
            turned = (value * factor).T
            low, high = turned[:128], turned[128:]
            keep_ref[band, part] = jnp.where(core == 0, low, high)
            give_ref[band, part] = jnp.where(core == 0, high, low)


def product(place, lefts, rights):
    parts, width, shots = rights[0].shape[1:]
    bands = parts // 2
    receivers = 4 * width
    hbm = pl.BlockSpec(memory_space=pl.ANY)
    out = jax.ShapeDtypeStruct((bands, 2, shots, receivers), jnp.float32)
    return pl.pallas_call(
        functools.partial(product_kernel, bands=bands),
        out_shape=[out, out],
        in_specs=[pl.BlockSpec(memory_space=pltpu.SMEM)] + [hbm] * (len(lefts) + len(rights)),
        scratch_shapes=[
            pltpu.VMEM((8, parts, receivers, shots), jnp.bfloat16),
            pltpu.VMEM((2, parts, 4 * receivers, shots), jnp.bfloat16),
            pltpu.SemaphoreType.DMA((64,)),
        ],
        compiler_params=pltpu.CompilerParams(vmem_limit_bytes=32 * 1024 * 1024),
        cost_estimate=pl.CostEstimate(
            flops=8 * bands * receivers * receivers * 1024,
            bytes_accessed=24 << 20,
            transcendentals=0,
        ),
        name="product",
    )(place, *lefts, *rights)


def local(traces, ghost_filter, bands):
    plane = lax.axis_index("shot")
    column = lax.axis_index("rx")
    row = lax.axis_index("ry")
    core, chip = row % 2, row // 2
    place = jnp.stack([plane, core, chip, column]).astype(jnp.int32)
    planes = 8
    fronts = front(place, ghost_filter, bands, traces, CHUNKS, planes)
    mine, others = fronts[:CHUNKS], fronts[CHUNKS:]

    def along_x(value, hop):
        pairs = [(i, ((i // 2 + hop) % 4) * 2 + i % 2) for i in range(8)]
        return lax.ppermute(value, "ry", pairs)

    def along_y(value, hop):
        return lax.ppermute(value, "rx", [(i, (i + hop) % 4) for i in range(4)])

    def along_z(value, hop):
        return lax.ppermute(value, "shot", [(i, (i + hop) % planes) for i in range(planes)])

    def swap(value):
        return lax.ppermute(value, "ry", [(i, i ^ 1) for i in range(8)])

    keeps, takes = [], []
    for chunk in range(CHUNKS):
        own = mine[chunk]
        theirs = swap(others[chunk])
        low = jnp.where(core == 0, own, theirs)
        high = jnp.where(core == 0, theirs, own)
        pieces = [None] * planes
        for hop in ZORDER:
            piece = jnp.concatenate([low[hop], high[hop]], 1)
            pieces[hop] = along_z(piece, hop) if hop else piece
        held, own_turn, up_turn, far_turn, down_turn = sort_blocks(place, pieces)
        own_up, own_down = along_y(own_turn, 1), along_y(own_turn, -1)
        up_turn, down_turn, far_turn = (
            along_x(up_turn, 1),
            along_x(down_turn, -1),
            along_x(far_turn, 2),
        )
        up, down, turned = second_step(
            held, (up_turn, down_turn, far_turn), (own_up, own_down)
        )
        y_up, y_down = along_y(turned, 1), along_y(turned, -1)
        up, down = along_x(up, 1), along_x(down, -1)
        y_up_far, y_down_far, x_up_far, x_down_far = third_step(
            y_up, y_down, own_down, up, down
        )
        y_up_far, y_down_far = along_y(y_up_far, 1), along_y(y_down_far, -1)
        x_up_far, x_down_far = along_x(x_up_far, 1), along_x(x_down_far, -1)
        keep, give = product(
            place,
            (y_up_far, y_down_far, y_up, y_down, own_up, own_down, own_turn, turned),
            (held, up, down, x_up_far, x_down_far),
        )
        keeps.append(keep)
        takes.append(swap(give))
    return jnp.where(
        core == 0,
        jnp.concatenate(keeps + takes),
        jnp.concatenate(takes + keeps),
    )


def solution(mesh):
    placed = (P("shot", ("rx", "ry"), None), P(), P())
    return jax.shard_map(
        local, mesh=mesh, in_specs=placed, out_specs=P("shot", None, "ry", "rx"), check_vma=False
    )
```

```python
import functools
import math

import jax
import jax.numpy as jnp
from jax import lax
from jax.experimental import pallas as pl
from jax.experimental.pallas import tpu as pltpu
from jax.sharding import PartitionSpec as P

ZORDER = (7, 1, 6, 2, 3, 5, 4, 0)


def filter_table(taps_ref, bands_ref, weights_ref, table_ref):
    samples = weights_ref.shape[0]
    taps = taps_ref.shape[1]
    bands = bands_ref[...]
    count = bands.shape[1]
    both = jnp.concatenate([bands, bands], 1)
    first = lax.broadcasted_iota(jnp.int32, (1, 2 * count), 1) < count
    step = 32
    index = lax.broadcasted_iota(jnp.int32, (step, 2 * count), 0)

    def angle_of(times):
        phase = lax.rem(times * both, samples)
        return (2.0 * math.pi / samples) * phase.astype(jnp.float32)

    coarse = angle_of(index * step)
    fine = angle_of(index)
    coarse_cos, coarse_sin = jnp.cos(coarse), jnp.sin(coarse)
    scale = 1.0 / math.sqrt(samples)
    fine_cos, fine_sin = jnp.cos(fine) * scale, jnp.sin(fine) * scale
    first_part = jnp.where(first, coarse_cos, -coarse_sin)
    second_part = jnp.where(first, coarse_sin, coarse_cos)
    for block in range(samples // step):
        rows = (
            first_part[block : block + 1] * fine_cos - second_part[block : block + 1] * fine_sin
        )
        table_ref[block * step : (block + 1) * step, :] = rows.astype(jnp.bfloat16)
    table_ref[samples:, :] = jnp.zeros((table_ref.shape[0] - samples, 2 * count), jnp.bfloat16)

    block = 128
    padded = jnp.concatenate(
        [taps_ref[...].astype(jnp.float32), jnp.zeros((1, 2 * block - taps), jnp.float32)], 1
    )
    band_matrix = pltpu.roll(
        jnp.broadcast_to(padded, (block, 2 * block)), 0, 1, stride=1, stride_axis=0
    ).astype(jnp.bfloat16)
    for at in range(samples // block):
        filtered = jnp.dot(
            band_matrix,
            table_ref[at * block : (at + 2) * block, :],
            preferred_element_type=jnp.float32,
        )
        high = filtered.astype(jnp.bfloat16)
        low = (filtered - high.astype(jnp.float32)).astype(jnp.bfloat16)
        weights_ref[at * block : (at + 1) * block, : 2 * count] = high
        weights_ref[at * block : (at + 1) * block, 2 * count :] = low


def front_kernel(taps_ref, bands_ref, traces_ref, *rest, planes, block, parts, pitch):
    mine, others = rest[:2]
    weights_ref, table_ref, traces, picked, turned, sems = rest[2:]
    shots, receivers, samples = traces_ref.shape
    count = bands_ref.shape[1]
    lanes = 2 * count
    size = shots // parts
    blocks = receivers // block

    def load(at, part):
        rows = pl.ds(part * size, size)
        return pltpu.make_async_copy(
            traces_ref.at[rows, pl.ds(at * block, block), :],
            traces.at[at, rows],
            sems.at[at, part],
        )

    for at in range(blocks):
        for part in range(parts):
            load(at, part).start()
    filter_table(taps_ref, bands_ref, weights_ref, table_ref)

    group = 256 // block

    def pick(at, part):
        load(at, part).wait()
        for first in range(part * size, (part + 1) * size, group):
            rows = traces[at, first : first + group].reshape(group * block, samples)
            both = jnp.dot(rows, weights_ref[...], preferred_element_type=jnp.float32)
            picked[at, first * block : (first + group) * block, :] = (
                both[:, :lanes] + both[:, lanes:]
            )

    def turn(at, receiver):
        turned[at, receiver * pitch : receiver * pitch + lanes, :] = picked[
            at, pl.ds(receiver, shots, stride=block), :
        ].T

    plane, core, _, _ = place_of()
    owned = count // planes
    half = owned // 2

    def write(at, hop):
        for other, out in enumerate((mine, others)):
            base = lax.rem(plane + hop, planes) * owned + (core ^ other) * half
            for part in range(2):
                for band in range(half):
                    rows = turned[
                        at, pl.ds(base + (part * count + band), block, stride=pitch), :
                    ]
                    out[hop, part * half + band, at * block : (at + 1) * block, :] = rows.astype(
                        jnp.bfloat16
                    )

    for at in range(blocks + 1):
        for part in range(parts):
            if at < blocks:
                pick(at, part)
            if at > 0 and part < parts // 2:
                step = 2 * block // parts
                for receiver in range(part * step, (part + 1) * step):
                    turn(at - 1, receiver)
            elif at > 0:
                step = 2 * planes // parts
                for hop in range((part - parts // 2) * step, (part - parts // 2 + 1) * step):
                    write(at - 1, hop)


def front(taps, bands, traces, planes):
    shots, receivers, samples = traces.shape
    count = bands.shape[0]
    block, parts = 16, 2
    pitch = 2 * count + 4
    blocks = receivers // block
    out = jax.ShapeDtypeStruct((planes, count // planes, receivers, shots), jnp.bfloat16)
    vmem = pl.BlockSpec(memory_space=pltpu.VMEM)
    return pl.pallas_call(
        functools.partial(front_kernel, planes=planes, block=block, parts=parts, pitch=pitch),
        out_shape=[out] * 2,
        grid=(1,),
        in_specs=[
            pl.BlockSpec((1, taps.shape[0]), lambda i: (0, 0)),
            pl.BlockSpec((1, count), lambda i: (0, 0)),
            pl.BlockSpec(memory_space=pltpu.HBM),
        ],
        out_specs=[vmem] * 2,
        scratch_shapes=[
            pltpu.VMEM((samples, 4 * count), jnp.bfloat16),
            pltpu.VMEM((samples + 128, 2 * count), jnp.bfloat16),
            pltpu.VMEM((blocks, shots, block, samples), jnp.bfloat16),
            pltpu.VMEM((blocks, shots * block, 2 * count), jnp.float32),
            pltpu.VMEM((blocks, block * pitch, shots), jnp.float32),
            pltpu.SemaphoreType.DMA((blocks, parts)),
        ],
        compiler_params=pltpu.CompilerParams(vmem_limit_bytes=52 * 1024 * 1024),
        cost_estimate=pl.CostEstimate(
            flops=4 * shots * receivers * samples * count * 2,
            bytes_accessed=shots * receivers * samples * 2,
            transcendentals=0,
        ),
        name="front",
    )(taps.reshape(1, -1), bands.reshape(1, -1), traces)


UP = ((6, 2), (0, 2), (4, 2))
DOWN = ((1, 3), (0, 1), (4, 2))


def place_of():
    row = lax.axis_index("ry")
    return lax.axis_index("shot"), lax.rem(row, 2), row // 2, lax.axis_index("rx")


def sort_kernel(*refs):
    pieces = refs[:8]
    held = refs[8]
    turns = refs[9:]
    plane, core, chip, _ = place_of()
    first = plane - 2 * chip + 8
    width = held.shape[2] // 2
    for hop, piece in zip(ZORDER, pieces):
        block = lax.rem(first - hop + 8, 8)
        for part in range(2):
            start = pl.multiple_of((core ^ part) * width, width)
            held[block, :, pl.ds(start, width), :] = piece[:, part * width : (part + 1) * width]
    for pair, turn in enumerate(turns):
        turn[...] = held[2 * pair : 2 * pair + 2]


def sort_blocks(pieces):
    shape = pieces[0].shape
    two = jax.ShapeDtypeStruct((2,) + shape, jnp.bfloat16)
    eight = jax.ShapeDtypeStruct((8,) + shape, jnp.bfloat16)
    vmem = pl.BlockSpec(memory_space=pltpu.VMEM)
    return pl.pallas_call(
        sort_kernel,
        out_shape=[eight, two, two, two, two],
        in_specs=[vmem] * 8,
        out_specs=[vmem] * 5,
        compiler_params=pltpu.CompilerParams(vmem_limit_bytes=16 * 1024 * 1024),
        cost_estimate=pl.CostEstimate(flops=0, bytes_accessed=1 << 20, transcendentals=0),
        name="sort",
    )(*[pieces[hop] for hop in ZORDER])


def second_kernel(held, after_up, after_down, up_turn, down_turn, far_turn, up, down, turned):
    del after_up, after_down
    for target, order in ((up, UP), (down, DOWN)):
        at = 0
        for first, size in order:
            target[at : at + size] = held[first : first + size]
            at += size
    for at, turn in enumerate((up_turn, down_turn, far_turn)):
        turned[at] = turn[...]


def second_step(held, turns, after):
    block = held.shape[1:]
    six = jax.ShapeDtypeStruct((6,) + block, jnp.bfloat16)
    turned = jax.ShapeDtypeStruct((3, 2) + block, jnp.bfloat16)
    vmem = pl.BlockSpec(memory_space=pltpu.VMEM)
    hbm = pl.BlockSpec(memory_space=pl.ANY)
    return pl.pallas_call(
        second_kernel,
        out_shape=[six, six, turned],
        in_specs=[vmem] + [hbm] * 2 + [vmem] * 3,
        out_specs=[vmem] * 3,
        compiler_params=pltpu.CompilerParams(vmem_limit_bytes=16 * 1024 * 1024),
        cost_estimate=pl.CostEstimate(flops=0, bytes_accessed=1 << 20, transcendentals=0),
        name="second",
    )(held, *after, *turns)


def third_kernel(y_up, y_down, own_down, x_up, x_down, y_up_far, y_down_far, x_up_far, x_down_far):
    y_up_far[...] = y_up[:2]
    y_down_far[0] = own_down[...]
    y_down_far[1] = y_down[2]
    x_up_far[...] = x_up[:3]
    x_down_far[...] = x_down[:3]


def third_step(y_up, y_down, own_down, x_up, x_down):
    block = x_up.shape[1:]
    two = jax.ShapeDtypeStruct((2, 2) + block, jnp.bfloat16)
    three = jax.ShapeDtypeStruct((3,) + block, jnp.bfloat16)
    vmem = pl.BlockSpec(memory_space=pltpu.VMEM)
    return pl.pallas_call(
        third_kernel,
        out_shape=[two, two, three, three],
        in_specs=[vmem] * 5,
        out_specs=[vmem] * 4,
        compiler_params=pltpu.CompilerParams(vmem_limit_bytes=16 * 1024 * 1024),
        cost_estimate=pl.CostEstimate(flops=0, bytes_accessed=1 << 20, transcendentals=0),
        name="third",
    )(y_up, y_down, own_down, x_up, x_down)


LEFTS = (
    (3, (0,)),
    (1, (0,)),
    (3, (1, 2, 3)),
    (1, (1, 2, 3)),
    (0, (0,)),
    (0, (1, 2, 3)),
)
LAST_LEFTS = ((2, (1, 2)), (2, (0, 3)))


def panel_copies(right, left, sems, rights, lefts):
    _, _, chip, column = place_of()
    width = right.shape[2] // 4
    chips = [lax.rem(chip + hop, 4) for hop in (0, 3, 1, 2)]
    copies = []

    def copy(source, target):
        copies.append(pltpu.make_async_copy(source, target, sems.at[len(copies)]))

    for source, runs, slot in rights:
        at = 0
        for first, size in runs:
            while size and at < source.shape[0]:
                step = min(size, 2 - first % 2, source.shape[0] - at)
                block = lax.rem(2 * chips[slot] + first, 8)
                start = pl.multiple_of(chips[slot] * width, width)
                copy(
                    source.at[pl.ds(at, step)],
                    right.at[pl.ds(block, step), :, pl.ds(start, width), :],
                )
                at, first, size = at + step, first + step, size - step
    for source, (hop, slots) in lefts:
        for at, slot in enumerate(slots):
            start = lax.rem(column + hop, 4) * 4 * width + chips[slot] * width
            copy(
                source.at[at] if len(slots) > 1 else source,
                left.at[:, :, pl.ds(pl.multiple_of(start, width), width), :],
            )
    for one in copies:
        one.start()
    for one in copies:
        one.wait()


def stage_kernel(*refs):
    lefts = refs[: len(LEFTS)]
    held, up, down = refs[len(LEFTS) : len(LEFTS) + 3]
    right, left, sems = refs[len(LEFTS) + 3 :]
    turned = lefts[-1]
    rights = [(held, ((0, 8),), 0), (up, UP, 1), (down, DOWN, 2)]
    for slot, first in ((1, 2), (2, 6), (3, 4)):
        rights.append((turned.at[slot - 1], ((first, 2),), slot))
    panel_copies(right, left, sems, rights, list(zip(lefts, LEFTS)))


def stage(lefts, rights):
    blocks, parts, width, shots = rights[0].shape
    anywhere = pl.BlockSpec(memory_space=pl.ANY)
    vmem = pl.BlockSpec(memory_space=pltpu.VMEM)
    return pl.pallas_call(
        stage_kernel,
        out_shape=[
            jax.ShapeDtypeStruct((blocks, parts, 4 * width, shots), jnp.bfloat16),
            jax.ShapeDtypeStruct((2, parts, 16 * width, shots), jnp.bfloat16),
        ],
        in_specs=[anywhere] * (len(lefts) + len(rights)),
        out_specs=[vmem] * 2,
        scratch_shapes=[pltpu.SemaphoreType.DMA((64,))],
        compiler_params=pltpu.CompilerParams(vmem_limit_bytes=16 * 1024 * 1024),
        cost_estimate=pl.CostEstimate(flops=0, bytes_accessed=8 << 20, transcendentals=0),
        name="stage",
    )(*lefts, *rights)


def multiply(right, left, keep, give, out, out_sem, bands):
    _, core, _, _ = place_of()
    half_bands = right.shape[1] // 2
    factor = -1.0 / math.sqrt(left.shape[2])
    stores = []
    for at, band in enumerate(bands):
        rows = jnp.concatenate(
            [
                jnp.concatenate(
                    [right[z, part * half_bands + band] for z in range(right.shape[0])], 1
                )
                for part in range(2)
            ],
            0,
        )
        real, imag = (
            jnp.dot(
                rows,
                jnp.concatenate(
                    [left[s, part * half_bands + band] for s in (core, 1 - core)], 1
                ),
                preferred_element_type=jnp.float32,
            )
            for part in range(2)
        )
        half = real.shape[0] // 2
        for part, value in enumerate((real[:half] - imag[half:], imag[:half] + real[half:])):
            turned_value = (value * factor).T
            keep[at, part] = turned_value[: half // 2]
            give[at, part] = turned_value[half // 2 :]
        store = pltpu.make_async_copy(
            keep.at[at], out.at[core * half_bands + band], out_sem.at[at]
        )
        store.start()
        stores.append(store)
    for store in stores:
        store.wait()


def first_product_kernel(*refs, bands):
    y_up_far, y_down_far, x_up_far, x_down_far = refs[2:6]
    right, left, out, give, keep, sems, out_sem = refs[6:]
    panel_copies(
        right,
        left,
        sems,
        [(x_up_far, UP, 3), (x_down_far, DOWN, 3)],
        list(zip((y_up_far, y_down_far), LAST_LEFTS)),
    )
    multiply(right, left, keep, give, out, out_sem, bands)


def second_product_kernel(right, left, _, out, give, keep, out_sem, *, bands):
    multiply(right, left, keep, give, out, out_sem, bands)


def product_cost(right, left, bands):
    return pl.CostEstimate(
        flops=8 * len(bands) * right.shape[2] * 2 * left.shape[3] * left.shape[2],
        bytes_accessed=8 << 20,
        transcendentals=0,
    )


def first_product(right, left, last, bands):
    vmem = pl.BlockSpec(memory_space=pltpu.VMEM)
    block = (2, left.shape[3], right.shape[2])
    return pl.pallas_call(
        functools.partial(first_product_kernel, bands=bands),
        out_shape=[
            jax.ShapeDtypeStruct(right.shape, right.dtype),
            jax.ShapeDtypeStruct(left.shape, left.dtype),
            jax.ShapeDtypeStruct((right.shape[1],) + block, jnp.float32),
            jax.ShapeDtypeStruct((len(bands),) + block, jnp.float32),
        ],
        in_specs=[vmem] * 2 + [pl.BlockSpec(memory_space=pl.ANY)] * 4,
        out_specs=[vmem, vmem, pl.BlockSpec(memory_space=pltpu.HBM), vmem],
        scratch_shapes=[
            pltpu.VMEM((len(bands),) + block, jnp.float32),
            pltpu.SemaphoreType.DMA((16,)),
            pltpu.SemaphoreType.DMA((len(bands),)),
        ],
        input_output_aliases={0: 0, 1: 1},
        compiler_params=pltpu.CompilerParams(vmem_limit_bytes=32 * 1024 * 1024),
        cost_estimate=product_cost(right, left, bands),
        name="first_product",
    )(right, left, *last)


def second_product(right, left, whole, bands):
    vmem = pl.BlockSpec(memory_space=pltpu.VMEM)
    hbm = pl.BlockSpec(memory_space=pltpu.HBM)
    block = (2, left.shape[3], right.shape[2])
    return pl.pallas_call(
        functools.partial(second_product_kernel, bands=bands),
        out_shape=[
            jax.ShapeDtypeStruct(whole.shape, whole.dtype),
            jax.ShapeDtypeStruct((len(bands),) + block, jnp.float32),
        ],
        in_specs=[vmem, vmem, hbm],
        out_specs=[hbm, vmem],
        scratch_shapes=[
            pltpu.VMEM((len(bands),) + block, jnp.float32),
            pltpu.SemaphoreType.DMA((len(bands),)),
        ],
        input_output_aliases={2: 0},
        compiler_params=pltpu.CompilerParams(vmem_limit_bytes=32 * 1024 * 1024),
        cost_estimate=product_cost(right, left, bands),
        name="second_product",
    )(right, left, whole)


def local(traces, ghost_filter, bands):
    planes = 8
    mine, others = front(ghost_filter, bands, traces, planes)

    def along_x(value, hop):
        pairs = [(i, ((i // 2 + hop) % 4) * 2 + i % 2) for i in range(8)]
        return lax.ppermute(value, "ry", pairs)

    def along_y(value, hop):
        return lax.ppermute(value, "rx", [(i, (i + hop) % 4) for i in range(4)])

    def along_z(value, hop):
        return lax.ppermute(value, "shot", [(i, (i + hop) % planes) for i in range(planes)])

    def swap(value):
        return lax.ppermute(value, "ry", [(i, i ^ 1) for i in range(8)])

    theirs = swap(others)
    pieces = [None] * planes
    for hop in ZORDER:
        piece = jnp.concatenate([mine[hop], theirs[hop]], 1)
        pieces[hop] = along_z(piece, hop) if hop else piece
    held, own_turn, up_turn, far_turn, down_turn = sort_blocks(pieces)
    own_up, own_down = along_y(own_turn, 1), along_y(own_turn, -1)
    turns = along_x(up_turn, 1), along_x(down_turn, -1), along_x(far_turn, 2)
    up, down, turned = second_step(held, turns, (own_up, own_down))
    y_up, y_down = along_y(turned, 1), along_y(turned, -1)
    up, down = along_x(up, 1), along_x(down, -1)
    y_up_far, y_down_far, x_up_far, x_down_far = third_step(y_up, y_down, own_down, up, down)
    y_up_far, y_down_far = along_y(y_up_far, 1), along_y(y_down_far, -1)
    x_up_far, x_down_far = along_x(x_up_far, 1), along_x(x_down_far, -1)
    right, left = stage((own_up, own_down, y_up, y_down, own_turn, turned), (held, up, down))
    half = right.shape[1] // 4
    right, left, whole, first_give = first_product(
        right, left, (y_up_far, y_down_far, x_up_far, x_down_far), tuple(range(half))
    )
    first_take = swap(first_give)
    whole, second_give = second_product(right, left, whole, tuple(range(half, 2 * half)))
    second_take = swap(second_give)
    start = (1 - lax.rem(lax.axis_index("ry"), 2)) * 2 * half
    whole = lax.dynamic_update_slice(whole, first_take, (start, 0, 0, 0))
    return lax.dynamic_update_slice(whole, second_take, (start + half, 0, 0, 0))


def solution(mesh):
    placed = (P("shot", ("rx", "ry"), None), P(), P())
    return jax.shard_map(
        local, mesh=mesh, in_specs=placed, out_specs=P("shot", None, "ry", "rx"), check_vma=False
    )
```

```python
import functools
import math

import jax
import jax.numpy as jnp
from jax import lax
from jax.experimental import pallas as pl
from jax.experimental.pallas import tpu as pltpu
from jax.sharding import PartitionSpec as P

ZORDER = (7, 1, 6, 2, 3, 5, 4, 0)


def filter_table(small_ref, weights_ref, table_ref):
    samples = weights_ref.shape[0]
    small = small_ref[...]
    count = small.shape[1] // 2
    first = lax.broadcasted_iota(jnp.int32, (1, 2 * count), 1) < count
    both = jnp.where(first, pltpu.roll(small, count, 1), small).astype(jnp.int32)
    step = 32
    index = lax.broadcasted_iota(jnp.int32, (step, 2 * count), 0)

    def angle_of(times):
        phase = lax.rem(times * both, samples)
        return (2.0 * math.pi / samples) * phase.astype(jnp.float32)

    coarse = angle_of(index * step)
    fine = angle_of(index)
    coarse_cos, coarse_sin = jnp.cos(coarse), jnp.sin(coarse)
    scale = 1.0 / math.sqrt(samples)
    fine_cos, fine_sin = jnp.cos(fine) * scale, jnp.sin(fine) * scale
    first_part = jnp.where(first, coarse_cos, -coarse_sin)
    second_part = jnp.where(first, coarse_sin, coarse_cos)
    for block in range(samples // step):
        rows = (
            first_part[block : block + 1] * fine_cos - second_part[block : block + 1] * fine_sin
        )
        table_ref[block * step : (block + 1) * step, :] = rows.astype(jnp.bfloat16)
    table_ref[samples:, :] = jnp.zeros((table_ref.shape[0] - samples, 2 * count), jnp.bfloat16)

    block = 128
    padded = jnp.concatenate(
        [jnp.where(first, small, 0.0), jnp.zeros((1, 2 * block - 2 * count), jnp.float32)], 1
    )
    band_matrix = pltpu.roll(
        jnp.broadcast_to(padded, (block, 2 * block)), 0, 1, stride=1, stride_axis=0
    ).astype(jnp.bfloat16)
    for at in range(samples // block):
        filtered = jnp.dot(
            band_matrix,
            table_ref[at * block : (at + 2) * block, :],
            preferred_element_type=jnp.float32,
        )
        high = filtered.astype(jnp.bfloat16)
        low = (filtered - high.astype(jnp.float32)).astype(jnp.bfloat16)
        weights_ref[at * block : (at + 1) * block, : 2 * count] = high
        weights_ref[at * block : (at + 1) * block, 2 * count :] = low


def front_kernel(small_ref, traces_ref, *rest, planes, block, parts, pitch):
    mine, others = rest[:2]
    weights_ref, table_ref, traces, picked, turned, sems = rest[2:]
    shots, receivers, samples = traces_ref.shape
    count = small_ref.shape[1] // 2
    lanes = 2 * count
    size = shots // parts
    blocks = receivers // block

    def load(at, part):
        rows = pl.ds(part * size, size)
        return pltpu.make_async_copy(
            traces_ref.at[rows, pl.ds(at * block, block), :],
            traces.at[at, rows],
            sems.at[at, part],
        )

    for at in range(blocks):
        for part in range(parts):
            load(at, part).start()
    filter_table(small_ref, weights_ref, table_ref)

    group = 256 // block

    def pick(at, part):
        load(at, part).wait()
        for first in range(part * size, (part + 1) * size, group):
            rows = traces[at, first : first + group].reshape(group * block, samples)
            both = jnp.dot(rows, weights_ref[...], preferred_element_type=jnp.float32)
            picked[at, first * block : (first + group) * block, :] = (
                both[:, :lanes] + both[:, lanes:]
            )

    def turn(at, receiver):
        turned[at, receiver * pitch : receiver * pitch + lanes, :] = picked[
            at, pl.ds(receiver, shots, stride=block), :
        ].T

    plane, core, _, _ = place_of()
    owned = count // planes
    half = owned // 2

    def write(at, hop):
        for other, out in enumerate((mine, others)):
            base = lax.rem(plane + hop, planes) * owned + (core ^ other) * half
            for part in range(2):
                for band in range(half):
                    rows = turned[
                        at, pl.ds(base + (part * count + band), block, stride=pitch), :
                    ]
                    out[hop, part * half + band, at * block : (at + 1) * block, :] = rows.astype(
                        jnp.bfloat16
                    )

    for at in range(blocks + 1):
        for part in range(parts):
            if at < blocks:
                pick(at, part)
            if at > 0 and part < parts // 2:
                step = 2 * block // parts
                for receiver in range(part * step, (part + 1) * step):
                    turn(at - 1, receiver)
            elif at > 0:
                step = 2 * planes // parts
                for hop in range((part - parts // 2) * step, (part - parts // 2 + 1) * step):
                    write(at - 1, hop)


def front(taps, bands, traces, planes):
    shots, receivers, samples = traces.shape
    count = bands.shape[0]
    block, parts = 16, 2
    pitch = 2 * count + 4
    blocks = receivers // block
    out = jax.ShapeDtypeStruct((planes, count // planes, receivers, shots), jnp.bfloat16)
    vmem = pl.BlockSpec(memory_space=pltpu.VMEM)
    return pl.pallas_call(
        functools.partial(front_kernel, planes=planes, block=block, parts=parts, pitch=pitch),
        out_shape=[out] * 2,
        in_specs=[
            vmem,
            pl.BlockSpec(memory_space=pltpu.HBM),
        ],
        out_specs=[vmem] * 2,
        scratch_shapes=[
            pltpu.VMEM((samples, 4 * count), jnp.bfloat16),
            pltpu.VMEM((samples + 128, 2 * count), jnp.bfloat16),
            pltpu.VMEM((blocks, shots, block, samples), jnp.bfloat16),
            pltpu.VMEM((blocks, shots * block, 2 * count), jnp.float32),
            pltpu.VMEM((blocks, block * pitch, shots), jnp.float32),
            pltpu.SemaphoreType.DMA((blocks, parts)),
        ],
        compiler_params=pltpu.CompilerParams(vmem_limit_bytes=52 * 1024 * 1024),
        cost_estimate=pl.CostEstimate(
            flops=4 * shots * receivers * samples * count * 2,
            bytes_accessed=shots * receivers * samples * 2,
            transcendentals=0,
        ),
        name="front",
    )(jnp.concatenate([taps.astype(jnp.float32), bands.astype(jnp.float32)]).reshape(1, -1), traces)


UP = ((6, 2), (0, 2), (4, 2))
DOWN = ((1, 3), (0, 1), (4, 2))


def place_of():
    row = lax.axis_index("ry")
    return lax.axis_index("shot"), lax.rem(row, 2), row // 2, lax.axis_index("rx")


def sort_kernel(*refs):
    pieces = refs[:8]
    held = refs[8]
    turns = refs[9:]
    plane, core, chip, _ = place_of()
    first = plane - 2 * chip + 8
    width = held.shape[2] // 2
    for hop, piece in zip(ZORDER, pieces):
        block = lax.rem(first - hop + 8, 8)
        for part in range(2):
            start = pl.multiple_of((core ^ part) * width, width)
            held[block, :, pl.ds(start, width), :] = piece[:, part * width : (part + 1) * width]
    for pair, turn in enumerate(turns):
        turn[...] = held[2 * pair : 2 * pair + 2]


def sort_blocks(pieces):
    shape = pieces[0].shape
    two = jax.ShapeDtypeStruct((2,) + shape, jnp.bfloat16)
    eight = jax.ShapeDtypeStruct((8,) + shape, jnp.bfloat16)
    vmem = pl.BlockSpec(memory_space=pltpu.VMEM)
    return pl.pallas_call(
        sort_kernel,
        out_shape=[eight, two, two, two, two],
        in_specs=[vmem] * 8,
        out_specs=[vmem] * 5,
        compiler_params=pltpu.CompilerParams(vmem_limit_bytes=16 * 1024 * 1024),
        cost_estimate=pl.CostEstimate(flops=0, bytes_accessed=1 << 20, transcendentals=0),
        name="sort",
    )(*[pieces[hop] for hop in ZORDER])


def second_kernel(held, own_up, own_down, down_turn, up_turn, far_turn, up, down, turned, owns):
    for target, order in ((up, UP), (down, DOWN)):
        at = 0
        for first, size in order:
            target[at : at + size] = held[first : first + size]
            at += size
    for at, turn in enumerate((up_turn, down_turn, far_turn)):
        turned[at] = turn[...]
    for at, own in enumerate((own_up, own_down)):
        owns[at] = own[...]


def second_step(held, turns, owns):
    block = held.shape[1:]
    six = jax.ShapeDtypeStruct((6,) + block, jnp.bfloat16)
    turned = jax.ShapeDtypeStruct((3, 2) + block, jnp.bfloat16)
    both = jax.ShapeDtypeStruct((2, 2) + block, jnp.bfloat16)
    vmem = pl.BlockSpec(memory_space=pltpu.VMEM)
    return pl.pallas_call(
        second_kernel,
        out_shape=[six, six, turned, both],
        in_specs=[vmem] * 6,
        out_specs=[vmem] * 4,
        compiler_params=pltpu.CompilerParams(vmem_limit_bytes=16 * 1024 * 1024),
        cost_estimate=pl.CostEstimate(flops=0, bytes_accessed=1 << 20, transcendentals=0),
        name="second",
    )(held, owns[0], owns[1], turns[1], turns[0], turns[2])


def third_kernel(y_up, y_down, x_up, owns, x_down, y_up_far, y_down_far, x_up_far, x_down_far):
    y_up_far[...] = y_up[:2]
    y_down_far[0] = owns[1]
    y_down_far[1] = y_down[2]
    x_up_far[...] = x_up[:3]
    x_down_far[...] = x_down[:3]


def third_step(y_up, y_down, owns, x_up, x_down):
    block = x_up.shape[1:]
    two = jax.ShapeDtypeStruct((2, 2) + block, jnp.bfloat16)
    three = jax.ShapeDtypeStruct((3,) + block, jnp.bfloat16)
    vmem = pl.BlockSpec(memory_space=pltpu.VMEM)
    return pl.pallas_call(
        third_kernel,
        out_shape=[two, two, three, three],
        in_specs=[vmem] * 5,
        out_specs=[vmem] * 4,
        compiler_params=pltpu.CompilerParams(vmem_limit_bytes=16 * 1024 * 1024),
        cost_estimate=pl.CostEstimate(flops=0, bytes_accessed=1 << 20, transcendentals=0),
        name="third",
    )(y_up, y_down, x_up, owns, x_down)


LEFTS = (
    (3, (1, 2, 3)),
    (1, (1, 2, 3)),
    (0, (0,)),
    (0, (1, 2, 3)),
)
LAST_LEFTS = ((2, (1, 2)), (2, (0, 3)))


def panel_copies(right, left, sems, rights, lefts):
    _, _, chip, column = place_of()
    width = right.shape[2] // 4
    chips = [lax.rem(chip + hop, 4) for hop in (0, 3, 1, 2)]
    copies = []

    def copy(source, target):
        copies.append(pltpu.make_async_copy(source, target, sems.at[len(copies)]))

    for source, runs, slot in rights:
        at = 0
        for first, size in runs:
            while size and at < source.shape[0]:
                step = min(size, 2 - first % 2, source.shape[0] - at)
                block = lax.rem(2 * chips[slot] + first, 8)
                start = pl.multiple_of(chips[slot] * width, width)
                copy(
                    source.at[pl.ds(at, step)],
                    right.at[pl.ds(block, step), :, pl.ds(start, width), :],
                )
                at, first, size = at + step, first + step, size - step
    for source, (hop, slots) in lefts:
        for at, slot in enumerate(slots):
            start = lax.rem(column + hop, 4) * 4 * width + chips[slot] * width
            copy(
                source.at[at] if len(slots) > 1 else source,
                left.at[:, :, pl.ds(pl.multiple_of(start, width), width), :],
            )
    for one in copies:
        one.start()
    for one in copies:
        one.wait()


def stage_kernel(*refs):
    lefts = refs[: len(LEFTS)]
    held, up, down = refs[len(LEFTS) : len(LEFTS) + 3]
    right, left, sems = refs[len(LEFTS) + 4 :]
    turned, owns = lefts[-1], refs[len(LEFTS) + 3]
    lefts = list(zip(lefts, LEFTS)) + [(owns.at[0], (3, (0,))), (owns.at[1], (1, (0,)))]
    rights = [(held, ((0, 8),), 0), (up, UP, 1), (down, DOWN, 2)]
    for slot, first in ((1, 2), (2, 6), (3, 4)):
        rights.append((turned.at[slot - 1], ((first, 2),), slot))
    panel_copies(right, left, sems, rights, lefts)


def stage(lefts, rights):
    blocks, parts, width, shots = rights[0].shape
    anywhere = pl.BlockSpec(memory_space=pl.ANY)
    vmem = pl.BlockSpec(memory_space=pltpu.VMEM)
    return pl.pallas_call(
        stage_kernel,
        out_shape=[
            jax.ShapeDtypeStruct((blocks, parts, 4 * width, shots), jnp.bfloat16),
            jax.ShapeDtypeStruct((2, parts, 16 * width, shots), jnp.bfloat16),
        ],
        in_specs=[anywhere] * (len(lefts) + len(rights)),
        out_specs=[vmem] * 2,
        scratch_shapes=[pltpu.SemaphoreType.DMA((64,))],
        compiler_params=pltpu.CompilerParams(vmem_limit_bytes=16 * 1024 * 1024),
        cost_estimate=pl.CostEstimate(flops=0, bytes_accessed=8 << 20, transcendentals=0),
        name="stage",
    )(*lefts, *rights)


def multiply(right, left, keep, give, bands):
    _, core, _, _ = place_of()
    half_bands = right.shape[1] // 2
    factor = -1.0 / math.sqrt(left.shape[2])
    for at, band in enumerate(bands):
        rows = jnp.concatenate(
            [
                jnp.concatenate(
                    [right[z, part * half_bands + band] for z in range(right.shape[0])], 1
                )
                for part in range(2)
            ],
            0,
        )
        real, imag = (
            jnp.dot(
                rows,
                jnp.concatenate(
                    [left[s, part * half_bands + band] for s in (core, 1 - core)], 1
                ),
                preferred_element_type=jnp.float32,
            )
            for part in range(2)
        )
        half = real.shape[0] // 2
        for part, value in enumerate((real[:half] - imag[half:], imag[:half] + real[half:])):
            turned_value = (value * factor).T
            keep[at, part] = turned_value[: half // 2]
            give[at, part] = turned_value[half // 2 :]


def first_product_kernel(*refs, bands):
    y_up_far, y_down_far, x_up_far, x_down_far = refs[2:6]
    right, left, keep, give, sems = refs[6:]
    panel_copies(
        right,
        left,
        sems,
        [(x_up_far, UP, 3), (x_down_far, DOWN, 3)],
        list(zip((y_up_far, y_down_far), LAST_LEFTS)),
    )
    multiply(right, left, keep, give, bands)


def second_product_kernel(right, left, keep, give, *, bands):
    multiply(right, left, keep, give, bands)


def product_cost(right, left, bands):
    return pl.CostEstimate(
        flops=8 * len(bands) * right.shape[2] * 2 * left.shape[3] * left.shape[2],
        bytes_accessed=8 << 20,
        transcendentals=0,
    )


def first_product(right, left, last, bands):
    vmem = pl.BlockSpec(memory_space=pltpu.VMEM)
    block = (2, left.shape[3], right.shape[2])
    return pl.pallas_call(
        functools.partial(first_product_kernel, bands=bands),
        out_shape=[
            jax.ShapeDtypeStruct(right.shape, right.dtype),
            jax.ShapeDtypeStruct(left.shape, left.dtype),
            jax.ShapeDtypeStruct((len(bands),) + block, jnp.float32),
            jax.ShapeDtypeStruct((len(bands),) + block, jnp.float32),
        ],
        in_specs=[vmem] * 2 + [pl.BlockSpec(memory_space=pl.ANY)] * 4,
        out_specs=[vmem] * 4,
        scratch_shapes=[pltpu.SemaphoreType.DMA((16,))],
        input_output_aliases={0: 0, 1: 1},
        compiler_params=pltpu.CompilerParams(vmem_limit_bytes=32 * 1024 * 1024),
        cost_estimate=product_cost(right, left, bands),
        name="first_product",
    )(right, left, *last)


def second_product(right, left, bands):
    vmem = pl.BlockSpec(memory_space=pltpu.VMEM)
    out = jax.ShapeDtypeStruct((len(bands), 2, left.shape[3], right.shape[2]), jnp.float32)
    return pl.pallas_call(
        functools.partial(second_product_kernel, bands=bands),
        out_shape=[out] * 2,
        in_specs=[vmem] * 2,
        out_specs=[vmem] * 2,
        compiler_params=pltpu.CompilerParams(vmem_limit_bytes=16 * 1024 * 1024),
        cost_estimate=product_cost(right, left, bands),
        name="second_product",
    )(right, left)


def local(traces, ghost_filter, bands):
    planes = 8
    mine, others = front(ghost_filter, bands, traces, planes)

    def along_x(value, hop):
        pairs = [(i, ((i // 2 + hop) % 4) * 2 + i % 2) for i in range(8)]
        return lax.ppermute(value, "ry", pairs)

    def along_y(value, hop):
        return lax.ppermute(value, "rx", [(i, (i + hop) % 4) for i in range(4)])

    def along_z(value, hop):
        return lax.ppermute(value, "shot", [(i, (i + hop) % planes) for i in range(planes)])

    def swap(value):
        return lax.ppermute(value, "ry", [(i, i ^ 1) for i in range(8)])

    theirs = swap(others)
    pieces = [None] * planes
    for hop in ZORDER:
        piece = jnp.concatenate([mine[hop], theirs[hop]], 1)
        pieces[hop] = along_z(piece, hop) if hop else piece
    held, own_turn, up_turn, far_turn, down_turn = sort_blocks(pieces)
    own_up, own_down = along_y(own_turn, 1), along_y(own_turn, -1)
    turns = along_x(up_turn, 1), along_x(down_turn, -1), along_x(far_turn, 2)
    up, down, turned, owns = second_step(held, turns, (own_up, own_down))
    y_up, y_down = along_y(turned, 1), along_y(turned, -1)
    up, down = along_x(up, 1), along_x(down, -1)
    y_up_far, y_down_far, x_up_far, x_down_far = third_step(y_up, y_down, owns, up, down)
    y_up_far, y_down_far = along_y(y_up_far, 1), along_y(y_down_far, -1)
    x_up_far, x_down_far = along_x(x_up_far, 1), along_x(x_down_far, -1)
    right, left = stage((y_up, y_down, own_turn, turned), (held, up, down, owns))
    half = right.shape[1] // 4
    right, left, first_keep, first_give = first_product(
        right, left, (y_up_far, y_down_far, x_up_far, x_down_far), tuple(range(half))
    )
    first_take = swap(first_give)
    second_keep, second_give = second_product(right, left, tuple(range(half, 2 * half)))
    keep = [first_keep, second_keep]
    take = [first_take, swap(second_give)]
    core = lax.rem(lax.axis_index("ry"), 2)
    low = [jnp.where(core == 0, k, t) for k, t in zip(keep, take)]
    high = [jnp.where(core == 0, t, k) for k, t in zip(keep, take)]
    return jnp.concatenate(low + high)


def solution(mesh):
    placed = (P("shot", ("rx", "ry"), None), P(), P())
    return jax.shard_map(
        local, mesh=mesh, in_specs=placed, out_specs=P("shot", None, "ry", "rx"), check_vma=False
    )
```

```python
import functools
import math

import jax
import jax.numpy as jnp
from jax import lax
from jax.experimental import pallas as pl
from jax.experimental.pallas import tpu as pltpu
from jax.sharding import PartitionSpec as P

ZORDER = (7, 1, 6, 2, 3, 5, 4, 0)


def filter_table(small_ref, weights_ref, table_ref):
    samples = weights_ref.shape[0]
    small = small_ref[...]
    count = small.shape[1] // 2
    first = lax.broadcasted_iota(jnp.int32, (1, 2 * count), 1) < count
    both = jnp.where(first, pltpu.roll(small, count, 1), small).astype(jnp.int32)
    step = 32
    index = lax.broadcasted_iota(jnp.int32, (step, 2 * count), 0)

    def angle_of(times):
        phase = lax.rem(times * both, samples)
        return (2.0 * math.pi / samples) * phase.astype(jnp.float32)

    coarse = angle_of(index * step)
    fine = angle_of(index)
    coarse_cos, coarse_sin = jnp.cos(coarse), jnp.sin(coarse)
    scale = 1.0 / math.sqrt(samples)
    fine_cos, fine_sin = jnp.cos(fine) * scale, jnp.sin(fine) * scale
    first_part = jnp.where(first, coarse_cos, -coarse_sin)
    second_part = jnp.where(first, coarse_sin, coarse_cos)
    for block in range(samples // step):
        rows = (
            first_part[block : block + 1] * fine_cos - second_part[block : block + 1] * fine_sin
        )
        table_ref[block * step : (block + 1) * step, :] = rows.astype(jnp.bfloat16)
    table_ref[samples:, :] = jnp.zeros((table_ref.shape[0] - samples, 2 * count), jnp.bfloat16)

    block = 128
    padded = jnp.concatenate(
        [jnp.where(first, small, 0.0), jnp.zeros((1, 2 * block - 2 * count), jnp.float32)], 1
    )
    band_matrix = pltpu.roll(
        jnp.broadcast_to(padded, (block, 2 * block)), 0, 1, stride=1, stride_axis=0
    ).astype(jnp.bfloat16)
    for at in range(samples // block):
        filtered = jnp.dot(
            band_matrix,
            table_ref[at * block : (at + 2) * block, :],
            preferred_element_type=jnp.float32,
        )
        high = filtered.astype(jnp.bfloat16)
        low = (filtered - high.astype(jnp.float32)).astype(jnp.bfloat16)
        weights_ref[at * block : (at + 1) * block, : 2 * count] = high
        weights_ref[at * block : (at + 1) * block, 2 * count :] = low


def front_kernel(small_ref, traces_ref, *rest, planes, block, parts, pitch):
    mine, others = rest[:2]
    weights_ref, table_ref, traces, picked, turned, sems = rest[2:]
    shots, receivers, samples = traces_ref.shape
    count = small_ref.shape[1] // 2
    lanes = 2 * count
    size = shots // parts
    blocks = receivers // block

    def load(at, part):
        rows = pl.ds(part * size, size)
        return pltpu.make_async_copy(
            traces_ref.at[rows, pl.ds(at * block, block), :],
            traces.at[at, rows],
            sems.at[at, part],
        )

    for at in range(blocks):
        for part in range(parts):
            load(at, part).start()
    filter_table(small_ref, weights_ref, table_ref)

    group = 256 // block

    def pick(at, part):
        load(at, part).wait()
        for first in range(part * size, (part + 1) * size, group):
            rows = traces[at, first : first + group].reshape(group * block, samples)
            both = jnp.dot(rows, weights_ref[...], preferred_element_type=jnp.float32)
            picked[at, first * block : (first + group) * block, :] = (
                both[:, :lanes] + both[:, lanes:]
            )

    def turn(at, receiver):
        turned[at, receiver * pitch : receiver * pitch + lanes, :] = picked[
            at, pl.ds(receiver, shots, stride=block), :
        ].T

    plane, core, _, _ = place_of()
    owned = count // planes
    half = owned // 2

    def write(at, hop):
        for other, out in enumerate((mine, others)):
            base = lax.rem(plane + hop, planes) * owned + (core ^ other) * half
            for part in range(2):
                for band in range(half):
                    rows = turned[
                        at, pl.ds(base + (part * count + band), block, stride=pitch), :
                    ]
                    out[hop, part * half + band, at * block : (at + 1) * block, :] = rows.astype(
                        jnp.bfloat16
                    )

    for at in range(blocks + 1):
        for part in range(parts):
            if at < blocks:
                pick(at, part)
            if at > 0 and part < parts // 2:
                step = 2 * block // parts
                for receiver in range(part * step, (part + 1) * step):
                    turn(at - 1, receiver)
            elif at > 0:
                step = 2 * planes // parts
                for hop in range((part - parts // 2) * step, (part - parts // 2 + 1) * step):
                    write(at - 1, hop)


def front(taps, bands, traces, planes):
    shots, receivers, samples = traces.shape
    count = bands.shape[0]
    block, parts = 16, 2
    pitch = 2 * count + 4
    blocks = receivers // block
    out = jax.ShapeDtypeStruct((planes, count // planes, receivers, shots), jnp.bfloat16)
    vmem = pl.BlockSpec(memory_space=pltpu.VMEM)
    return pl.pallas_call(
        functools.partial(front_kernel, planes=planes, block=block, parts=parts, pitch=pitch),
        out_shape=[out] * 2,
        in_specs=[
            vmem,
            pl.BlockSpec(memory_space=pltpu.HBM),
        ],
        out_specs=[vmem] * 2,
        scratch_shapes=[
            pltpu.VMEM((samples, 4 * count), jnp.bfloat16),
            pltpu.VMEM((samples + 128, 2 * count), jnp.bfloat16),
            pltpu.VMEM((blocks, shots, block, samples), jnp.bfloat16),
            pltpu.VMEM((blocks, (shots + 1) * block, 2 * count), jnp.float32),
            pltpu.VMEM((blocks, (block + 1) * pitch + 4, shots), jnp.float32),
            pltpu.SemaphoreType.DMA((blocks, parts)),
        ],
        compiler_params=pltpu.CompilerParams(vmem_limit_bytes=52 * 1024 * 1024),
        cost_estimate=pl.CostEstimate(
            flops=4 * shots * receivers * samples * count * 2,
            bytes_accessed=shots * receivers * samples * 2,
            transcendentals=0,
        ),
        name="front",
    )(jnp.concatenate([taps.astype(jnp.float32), bands.astype(jnp.float32)]).reshape(1, -1), traces)


UP = ((6, 2), (0, 2), (4, 2))
DOWN = ((1, 3), (0, 1), (4, 2))


def place_of():
    row = lax.axis_index("ry")
    return lax.axis_index("shot"), lax.rem(row, 2), row // 2, lax.axis_index("rx")


def sort_kernel(*refs):
    pieces = refs[:8]
    held = refs[8]
    turns = refs[9:]
    plane, core, chip, _ = place_of()
    first = plane - 2 * chip + 8
    width = held.shape[2] // 2
    for hop, piece in zip(ZORDER, pieces):
        block = lax.rem(first - hop + 8, 8)
        for part in range(2):
            start = pl.multiple_of((core ^ part) * width, width)
            held[block, :, pl.ds(start, width), :] = piece[:, part * width : (part + 1) * width]
    for pair, turn in enumerate(turns):
        turn[...] = held[2 * pair : 2 * pair + 2]


def sort_blocks(pieces):
    shape = pieces[0].shape
    two = jax.ShapeDtypeStruct((2,) + shape, jnp.bfloat16)
    eight = jax.ShapeDtypeStruct((8,) + shape, jnp.bfloat16)
    vmem = pl.BlockSpec(memory_space=pltpu.VMEM)
    return pl.pallas_call(
        sort_kernel,
        out_shape=[eight, two, two, two, two],
        in_specs=[vmem] * 8,
        out_specs=[vmem] * 5,
        compiler_params=pltpu.CompilerParams(vmem_limit_bytes=16 * 1024 * 1024),
        cost_estimate=pl.CostEstimate(flops=0, bytes_accessed=1 << 20, transcendentals=0),
        name="sort",
    )(*[pieces[hop] for hop in ZORDER])


def second_kernel(held, own_up, own_down, down_turn, up_turn, far_turn, up, down, turned, owns):
    for target, order in ((up, UP), (down, DOWN)):
        at = 0
        for first, size in order:
            target[at : at + size] = held[first : first + size]
            at += size
    for at, turn in enumerate((up_turn, down_turn, far_turn)):
        turned[at] = turn[...]
    for at, own in enumerate((own_up, own_down)):
        owns[at] = own[...]


def second_step(held, turns, owns):
    block = held.shape[1:]
    six = jax.ShapeDtypeStruct((6,) + block, jnp.bfloat16)
    turned = jax.ShapeDtypeStruct((3, 2) + block, jnp.bfloat16)
    both = jax.ShapeDtypeStruct((2, 2) + block, jnp.bfloat16)
    vmem = pl.BlockSpec(memory_space=pltpu.VMEM)
    return pl.pallas_call(
        second_kernel,
        out_shape=[six, six, turned, both],
        in_specs=[vmem] * 6,
        out_specs=[vmem] * 4,
        compiler_params=pltpu.CompilerParams(vmem_limit_bytes=16 * 1024 * 1024),
        cost_estimate=pl.CostEstimate(flops=0, bytes_accessed=1 << 20, transcendentals=0),
        name="second",
    )(held, owns[0], owns[1], turns[1], turns[0], turns[2])


def third_kernel(y_up, y_down, x_up, owns, x_down, y_up_far, y_down_far, x_up_far, x_down_far):
    y_up_far[...] = y_up[:2]
    y_down_far[0] = owns[1]
    y_down_far[1] = y_down[2]
    x_up_far[...] = x_up[:3]
    x_down_far[...] = x_down[:3]


def third_step(y_up, y_down, owns, x_up, x_down):
    block = x_up.shape[1:]
    two = jax.ShapeDtypeStruct((2, 2) + block, jnp.bfloat16)
    three = jax.ShapeDtypeStruct((3,) + block, jnp.bfloat16)
    vmem = pl.BlockSpec(memory_space=pltpu.VMEM)
    return pl.pallas_call(
        third_kernel,
        out_shape=[two, two, three, three],
        in_specs=[vmem] * 5,
        out_specs=[vmem] * 4,
        compiler_params=pltpu.CompilerParams(vmem_limit_bytes=16 * 1024 * 1024),
        cost_estimate=pl.CostEstimate(flops=0, bytes_accessed=1 << 20, transcendentals=0),
        name="third",
    )(y_up, y_down, x_up, owns, x_down)


LEFTS = (
    (3, (1, 2, 3)),
    (1, (1, 2, 3)),
    (0, (0,)),
    (0, (1, 2, 3)),
)
LAST_LEFTS = ((2, (1, 2)), (2, (0, 3)))


def panel_copies(right, left, sems, rights, lefts):
    _, _, chip, column = place_of()
    width = right.shape[2] // 4
    chips = [lax.rem(chip + hop, 4) for hop in (0, 3, 1, 2)]
    copies = []

    def copy(source, target):
        copies.append(pltpu.make_async_copy(source, target, sems.at[len(copies)]))

    for source, runs, slot in rights:
        at = 0
        for first, size in runs:
            while size and at < source.shape[0]:
                step = min(size, 2 - first % 2, source.shape[0] - at)
                block = lax.rem(2 * chips[slot] + first, 8)
                start = pl.multiple_of(chips[slot] * width, width)
                copy(
                    source.at[pl.ds(at, step)],
                    right.at[pl.ds(block, step), :, pl.ds(start, width), :],
                )
                at, first, size = at + step, first + step, size - step
    for source, (hop, slots) in lefts:
        for at, slot in enumerate(slots):
            start = lax.rem(column + hop, 4) * 4 * width + chips[slot] * width
            copy(
                source.at[at] if len(slots) > 1 else source,
                left.at[:, :, pl.ds(pl.multiple_of(start, width), width), :],
            )
    for one in copies:
        one.start()
    for one in copies:
        one.wait()


def stage_kernel(*refs):
    lefts = refs[: len(LEFTS)]
    held, up, down = refs[len(LEFTS) : len(LEFTS) + 3]
    right, left, sems = refs[len(LEFTS) + 4 :]
    turned, owns = lefts[-1], refs[len(LEFTS) + 3]
    lefts = list(zip(lefts, LEFTS)) + [(owns.at[0], (3, (0,))), (owns.at[1], (1, (0,)))]
    rights = [(held, ((0, 8),), 0), (up, UP, 1), (down, DOWN, 2)]
    for slot, first in ((1, 2), (2, 6), (3, 4)):
        rights.append((turned.at[slot - 1], ((first, 2),), slot))
    panel_copies(right, left, sems, rights, lefts)


def stage(lefts, rights):
    blocks, parts, width, shots = rights[0].shape
    anywhere = pl.BlockSpec(memory_space=pl.ANY)
    vmem = pl.BlockSpec(memory_space=pltpu.VMEM)
    return pl.pallas_call(
        stage_kernel,
        out_shape=[
            jax.ShapeDtypeStruct((blocks, parts, 4 * width, shots), jnp.bfloat16),
            jax.ShapeDtypeStruct((2, parts, 16 * width, shots), jnp.bfloat16),
        ],
        in_specs=[anywhere] * (len(lefts) + len(rights)),
        out_specs=[vmem] * 2,
        scratch_shapes=[pltpu.SemaphoreType.DMA((64,))],
        compiler_params=pltpu.CompilerParams(vmem_limit_bytes=16 * 1024 * 1024),
        cost_estimate=pl.CostEstimate(flops=0, bytes_accessed=8 << 20, transcendentals=0),
        name="stage",
    )(*lefts, *rights)


def multiply(right, left, keep, give, bands):
    _, core, _, _ = place_of()
    half_bands = right.shape[1] // 2
    factor = -1.0 / math.sqrt(left.shape[2])
    for at, band in enumerate(bands):
        rows = jnp.concatenate(
            [
                jnp.concatenate(
                    [right[z, part * half_bands + band] for z in range(right.shape[0])], 1
                )
                for part in range(2)
            ],
            0,
        )
        real, imag = (
            jnp.dot(
                rows,
                jnp.concatenate(
                    [left[s, part * half_bands + band] for s in (core, 1 - core)], 1
                ),
                preferred_element_type=jnp.float32,
            )
            for part in range(2)
        )
        half = real.shape[0] // 2
        for part, value in enumerate((real[:half] - imag[half:], imag[:half] + real[half:])):
            turned_value = (value * factor).T
            keep[at, part] = turned_value[: half // 2]
            give[at, part] = turned_value[half // 2 :]


def first_product_kernel(*refs, bands):
    y_up_far, y_down_far, x_up_far, x_down_far = refs[2:6]
    right, left, keep, give, sems = refs[6:]
    panel_copies(
        right,
        left,
        sems,
        [(x_up_far, UP, 3), (x_down_far, DOWN, 3)],
        list(zip((y_up_far, y_down_far), LAST_LEFTS)),
    )
    multiply(right, left, keep, give, bands)


def second_product_kernel(right, left, keep, give, *, bands):
    multiply(right, left, keep, give, bands)


def product_cost(right, left, bands):
    return pl.CostEstimate(
        flops=8 * len(bands) * right.shape[2] * 2 * left.shape[3] * left.shape[2],
        bytes_accessed=8 << 20,
        transcendentals=0,
    )


def first_product(right, left, last, bands):
    vmem = pl.BlockSpec(memory_space=pltpu.VMEM)
    block = (2, left.shape[3], right.shape[2])
    return pl.pallas_call(
        functools.partial(first_product_kernel, bands=bands),
        out_shape=[
            jax.ShapeDtypeStruct(right.shape, right.dtype),
            jax.ShapeDtypeStruct(left.shape, left.dtype),
            jax.ShapeDtypeStruct((len(bands),) + block, jnp.float32),
            jax.ShapeDtypeStruct((len(bands),) + block, jnp.float32),
        ],
        in_specs=[vmem] * 2 + [pl.BlockSpec(memory_space=pl.ANY)] * 4,
        out_specs=[vmem] * 4,
        scratch_shapes=[pltpu.SemaphoreType.DMA((16,))],
        input_output_aliases={0: 0, 1: 1},
        compiler_params=pltpu.CompilerParams(vmem_limit_bytes=32 * 1024 * 1024),
        cost_estimate=product_cost(right, left, bands),
        name="first_product",
    )(right, left, *last)


def second_product(right, left, bands):
    vmem = pl.BlockSpec(memory_space=pltpu.VMEM)
    out = jax.ShapeDtypeStruct((len(bands), 2, left.shape[3], right.shape[2]), jnp.float32)
    return pl.pallas_call(
        functools.partial(second_product_kernel, bands=bands),
        out_shape=[out] * 2,
        in_specs=[vmem] * 2,
        out_specs=[vmem] * 2,
        compiler_params=pltpu.CompilerParams(vmem_limit_bytes=16 * 1024 * 1024),
        cost_estimate=product_cost(right, left, bands),
        name="second_product",
    )(right, left)


def local(traces, ghost_filter, bands):
    planes = 8
    mine, others = front(ghost_filter, bands, traces, planes)

    def along_x(value, hop):
        pairs = [(i, ((i // 2 + hop) % 4) * 2 + i % 2) for i in range(8)]
        return lax.ppermute(value, "ry", pairs)

    def along_y(value, hop):
        return lax.ppermute(value, "rx", [(i, (i + hop) % 4) for i in range(4)])

    def along_z(value, hop):
        return lax.ppermute(value, "shot", [(i, (i + hop) % planes) for i in range(planes)])

    def swap(value):
        return lax.ppermute(value, "ry", [(i, i ^ 1) for i in range(8)])

    theirs = swap(others)
    pieces = [None] * planes
    for hop in ZORDER:
        piece = jnp.concatenate([mine[hop], theirs[hop]], 1)
        pieces[hop] = along_z(piece, hop) if hop else piece
    held, own_turn, up_turn, far_turn, down_turn = sort_blocks(pieces)
    own_up, own_down = along_y(own_turn, 1), along_y(own_turn, -1)
    turns = along_x(up_turn, 1), along_x(down_turn, -1), along_x(far_turn, 2)
    up, down, turned, owns = second_step(held, turns, (own_up, own_down))
    y_up, y_down = along_y(turned, 1), along_y(turned, -1)
    up, down = along_x(up, 1), along_x(down, -1)
    y_up_far, y_down_far, x_up_far, x_down_far = third_step(y_up, y_down, owns, up, down)
    y_up_far, y_down_far = along_y(y_up_far, 1), along_y(y_down_far, -1)
    x_up_far, x_down_far = along_x(x_up_far, 1), along_x(x_down_far, -1)
    right, left = stage((y_up, y_down, own_turn, turned), (held, up, down, owns))
    half = right.shape[1] // 4
    right, left, first_keep, first_give = first_product(
        right, left, (y_up_far, y_down_far, x_up_far, x_down_far), tuple(range(half))
    )
    first_take = swap(first_give)
    second_keep, second_give = second_product(right, left, tuple(range(half, 2 * half)))
    keep = [first_keep, second_keep]
    take = [first_take, swap(second_give)]
    core = lax.rem(lax.axis_index("ry"), 2)
    low = [jnp.where(core == 0, k, t) for k, t in zip(keep, take)]
    high = [jnp.where(core == 0, t, k) for k, t in zip(keep, take)]
    return jnp.concatenate(low + high)


def solution(mesh):
    placed = (P("shot", ("rx", "ry"), None), P(), P())
    return jax.shard_map(
        local, mesh=mesh, in_specs=placed, out_specs=P("shot", None, "ry", "rx"), check_vma=False
    )
```
